32 devices in a mesh: row: 4 (over y, core), stn: 2 (over x), chan: 4 (over z).
Axes of the slice: x: 2, y: 2, z: 4, core: 2. Of those that a mesh axis runs over, the one named last changes fastest.
Arguments:
- visibility: float32 [2, 4096, 640], P(None, ('chan', 'row', 'stn')), parts along dimension 1, may hold values from -0.5 to 0.5
- uv_offset: float32 [2, 4096, 640], P(None, ('chan', 'row', 'stn')), parts along dimension 1, may hold values from -12 to 12
- aterm: bfloat16 [2, 2048, 1024], P(None, ('chan', 'stn')), parts along dimension 1, may hold values from -4 to 4
- station_pair: int32 [4096, 2], P(('chan', 'row', 'stn')), parts along dimension 0, may hold values from 0 to 511
- tile_of: int32 [4096], P(('chan', 'row', 'stn')), parts along dimension 0, may hold values from 0 to 16383, as said below
- vis_count: int32 [4096], P(('chan', 'row', 'stn')), parts along dimension 0, may hold values from 1 to 640
Outputs:
- sky: float32 [8, 4096, 4096], P('chan', ('row', 'stn')), parts along dimension 0
The draws below stay inside these ranges and needn't reach their ends.
There are 4 independent parts, one for each index of `chan`. The reference program is written for one: setup_inputs(seed, part) draws one part's arguments, and reference() takes and returns one part's arrays. A program takes and returns all parts, laid end to end along the dimension named above; each array names one. Nothing has to cross between parts.
Inputs may be any that keep to these rules, and one draw needn't show every extreme that they name: `tile_of`: the owner of tile t is (t // 128 // 32) * 2 + (t % 128) // 64. Among the 128 subgrids of one device at most 32 have tiles of one owner, and in every draw some owner gets exactly 32 from every device.
All inputs are finite; a program needn't handle non-finite values.
Results may differ from the reference program's by a relative error of at most 0.0047.
Values may be sent and summed in bfloat16 or wider, within the bound.
A program may use at most 320 MiB of HBM per device.

```python
import math
import jax
import jax.numpy as jnp
from jax import lax

N = 4096
SUB = 32
STATIONS = 512
VIS = 640
S_DEV = 128
SUBGRIDS = 1024
CAP = 32
NT = 128
N_ROW = 4
N_STN = 2


def draw_tile_of(key, part):
    key = jax.random.fold_in(key, 7)
    owners = N_ROW * N_STN
    location_sequence = owners * CAP
    blocks = SUBGRIDS // S_DEV
    key_score, key_pick, key_row, key_col, key_order = jax.random.split(key, 5)
    station_chip_labels = jnp.arange(owners, dtype=jnp.int32)
    line_separation = jnp.abs(2 * (station_chip_labels // N_STN) - (N_ROW - 1)) * N_STN
    antenna_separation = jnp.abs(2 * (station_chip_labels % N_STN) - (N_STN - 1)) * N_ROW
    greatest_separation = (N_ROW - 1) * N_STN + (N_STN - 1) * N_ROW + 1
    nearness_gauge = (greatest_separation - line_separation - antenna_separation) * (32768 // greatest_separation)
    winning_candidate = jax.random.randint(key_pick, (), 0, owners)
    affinity_gain = nearness_gauge + jnp.where(station_chip_labels == winning_candidate, 524288, 0)
    location_slotting = jnp.arange(location_sequence, dtype=jnp.int32) // CAP
    noise_perturbation = jax.random.randint(key_score, (blocks, location_sequence), 0, 65536)
    sorting_key_quantity = (noise_perturbation + affinity_gain[location_slotting][None, :]) * location_sequence + jnp.arange(location_sequence, dtype=jnp.int32)[None, :]
    ignored, chosen = lax.top_k(sorting_key_quantity, S_DEV)
    shuffle = jax.random.randint(key_order, (blocks, S_DEV), 0, 65536) * S_DEV + jnp.arange(S_DEV, dtype=jnp.int32)[None, :]
    order = jnp.argsort(shuffle, axis=1)
    chosen = jnp.take_along_axis(chosen, order, axis=1)
    owner = chosen // CAP
    tile_rows = NT // N_ROW
    tile_cols = NT // N_STN
    row_inside = jax.random.randint(key_row, (blocks, S_DEV), 0, tile_rows)
    col_inside = jax.random.randint(key_col, (blocks, S_DEV), 0, tile_cols)
    tile_row = owner // N_STN * tile_rows + row_inside
    tile_col = owner % N_STN * tile_cols + col_inside
    return (tile_row * NT + tile_col).reshape(SUBGRIDS).astype(jnp.int32)


def set_ends(array, key, least, largest):
    longest = array.shape.index(max(array.shape))
    spots = []
    for shift in (0, 1):
        where = [jax.random.randint(jax.random.fold_in(key, axis), (), 0, length) for axis, length in enumerate(array.shape)]
        where[longest] = (where[longest] + shift) % array.shape[longest]
        spots.append(tuple(where))
    return array.at[spots[0]].set(least).at[spots[1]].set(largest)


def block_scale(own_key, shape, cuts, low, top_value):
    factor_of = 1.0
    for dim, shards_of in cuts:
        draws = jax.random.uniform(jax.random.fold_in(jax.random.fold_in(own_key, 6), dim), (shards_of,), jnp.float32, low / len(cuts), top_value / len(cuts))
        factor_of = factor_of * jnp.repeat(jnp.exp(draws), shape[dim] // shards_of).reshape((-1,) + (1,) * (len(shape) - 1 - dim))
    return factor_of


def normal_values(stream_key, extent, spread, most, cuts=(), held_as=jnp.bfloat16):
    drawn = jax.random.normal(stream_key, extent, jnp.float32) * spread
    if len(cuts) > 0:
        drawn = block_scale(stream_key, extent, cuts, -0.22, 0.18) * drawn
    return jnp.clip(drawn, min=-most, max=most).astype(held_as)


def setup_inputs(seed: int = 0, part: int = 0) -> dict:
    arg_keys = jax.random.split(jax.random.key(seed), 7)
    part_keys = jax.random.split(jax.random.fold_in(arg_keys[6], part), 7)
    return {
        "visibility": normal_values(part_keys[0], (2, SUBGRIDS, VIS), 0.0625, 0.5, ((1, 8),), jnp.float32),
        "uv_offset": jnp.clip(jax.random.uniform(part_keys[1], (2, SUBGRIDS, VIS), jnp.float32, -12.0, 12.0) * block_scale(part_keys[1], (2, SUBGRIDS, VIS), ((1, 8),), -0.4, 0.0), -12.0, 12.0),
        "aterm": normal_values(part_keys[2], (2, STATIONS, SUB * SUB), 0.7, 4.0, ((1, 2),)),
        "station_pair": set_ends(jax.random.randint(part_keys[3], (SUBGRIDS, 2), 0, STATIONS), jax.random.fold_in(part_keys[3], 1), 0, STATIONS - 1).astype(jnp.int32),
        "tile_of": draw_tile_of(jax.random.fold_in(jax.random.fold_in(arg_keys[6], part), 71), part),
        "vis_count": set_ends(jax.random.randint(part_keys[5], (SUBGRIDS,), 1, VIS + 1), jax.random.fold_in(part_keys[5], 1), 1, VIS).astype(jnp.int32),
    }


HIGHEST = lax.Precision.HIGHEST

def centred_table(length):
    offsets = jnp.arange(length, dtype=jnp.int32) - length // 2
    turns = jnp.mod(offsets[:, None] * offsets[None, :], length).astype(jnp.float32) * (2.0 * math.pi / length)
    factor = 1.0 / math.sqrt(length)
    return (jnp.cos(turns) * factor, -jnp.sin(turns) * factor)

def complex_contraction(pattern, left_re, left_im, right_re, right_im):
    real_part = jnp.einsum(pattern, left_re, right_re, precision=HIGHEST) - jnp.einsum(pattern, left_im, right_im, precision=HIGHEST)
    imag_part = jnp.einsum(pattern, left_re, right_im, precision=HIGHEST) + jnp.einsum(pattern, left_im, right_re, precision=HIGHEST)
    return (real_part, imag_part)

def rounded(value):
    return lax.optimization_barrier(value.astype(jnp.bfloat16)).astype(jnp.float32)

def subgrid_block(values_re, values_im, coord_u, coord_v, counts, first_re, first_im, second_re, second_im):
    side = SUB
    location_sequence = values_re.shape[1]
    pixels = (jnp.arange(side, dtype=jnp.float32) - side // 2) * (2.0 * math.pi / side)
    living = (jnp.arange(location_sequence, dtype=jnp.int32)[None, :] < counts[:, None]).astype(jnp.float32)
    values_re = values_re * living
    values_im = values_im * living
    angle_u = coord_u[:, None, :] * pixels[None, :, None]
    angle_v = coord_v[:, None, :] * pixels[None, :, None]
    cosine_u = jnp.cos(angle_u)
    sine_u = jnp.sin(angle_u)
    weighted_real = rounded(values_re[:, None, :] * cosine_u - values_im[:, None, :] * sine_u)
    weighted_imaginary = rounded(values_re[:, None, :] * sine_u + values_im[:, None, :] * cosine_u)
    image_real, image_imaginary = complex_contraction('hci,hzi->hcz', weighted_real, weighted_imaginary, rounded(jnp.cos(angle_v)), rounded(jnp.sin(angle_v)))
    batch = image_real.shape[0]
    beam_re = (first_re * second_re + first_im * second_im).reshape(batch, side, side)
    beam_im = (first_im * second_re - first_re * second_im).reshape(batch, side, side)
    shaped_re = image_real * beam_re - image_imaginary * beam_im
    shaped_im = image_real * beam_im + image_imaginary * beam_re
    table_re, table_im = centred_table(side)
    half_re, half_im = complex_contraction('ap,bpq->baq', table_re, table_im, shaped_re, shaped_im)
    full_re, full_im = complex_contraction('baq,cq->bac', half_re, half_im, table_re, table_im)
    joined = jnp.concatenate([full_re.reshape(batch, side * side), full_im.reshape(batch, side * side)], axis=1)
    return joined.astype(jnp.bfloat16)

def reference(visibility, uv_offset, aterm, station_pair, tile_of, vis_count):
    batch = math.gcd(SUBGRIDS, 256)

    def one_block(position):
        begin_at = (position * batch).astype(jnp.int32)
        values = lax.dynamic_slice_in_dim(visibility, begin_at, batch, 1)
        coords = lax.dynamic_slice_in_dim(uv_offset, begin_at, batch, 1)
        pairs = lax.dynamic_slice_in_dim(station_pair, begin_at, batch, 0)
        counts = lax.dynamic_slice_in_dim(vis_count, begin_at, batch, 0)
        first = jnp.take(aterm, pairs[:, 0], axis=1).astype(jnp.float32)
        second = jnp.take(aterm, pairs[:, 1], axis=1).astype(jnp.float32)
        return subgrid_block(values[0], values[1], coords[0], coords[1], counts, first[0], first[1], second[0], second[1])
    subgrids = lax.map(one_block, jnp.arange(SUBGRIDS // batch, dtype=jnp.int32)).reshape(SUBGRIDS, 2 * SUB * SUB)
    grid = jnp.zeros((NT * NT, 2 * SUB * SUB), jnp.float32).at[tile_of].add(subgrids.astype(jnp.float32))
    grid = grid.reshape(NT, NT, 2, SUB, SUB).transpose(2, 0, 3, 1, 4).reshape(2, N, N)
    image = jnp.fft.ifft2(grid[0] + 1j * grid[1]) * N
    swapped = image.T
    return jnp.stack([jnp.real(swapped), jnp.imag(swapped)]).astype(jnp.float32)
```

```python
import math

import jax
import jax.numpy as jnp
import ml_dtypes
import numpy as np
from jax import lax
from jax.experimental import pallas as pl
from jax.experimental.pallas import tpu as pltpu
from jax.sharding import PartitionSpec as P

N = 4096
SUB = 32
TILES = N // SUB
BF16 = jnp.bfloat16
F32 = jnp.float32

SIN_POLY = tuple((-1) ** k * math.pi ** (2 * k + 1) / math.factorial(2 * k + 1) for k in range(6))
COS_POLY = tuple((-1) ** k * math.pi ** (2 * k) / math.factorial(2 * k) for k in range(7))


def unit_circle(turns):
    part = turns - jnp.round(turns)
    square = part * part
    sine = SIN_POLY[-1]
    for coefficient in SIN_POLY[-2::-1]:
        sine = sine * square + coefficient
    sine = sine * part
    cosine = COS_POLY[-1]
    for coefficient in COS_POLY[-2::-1]:
        cosine = cosine * square + coefficient
    return 1.0 - 2.0 * sine * sine, 2.0 * sine * cosine


def split_high_low(table):
    high = table.astype(ml_dtypes.bfloat16)
    low = (table - high.astype(np.float64)).astype(ml_dtypes.bfloat16)
    return high, low


def predict_kernel(vis_ref, off_ref, count_ref, out_ref):
    subs, slots = vis_ref.shape[1], vis_ref.shape[2]
    slot = lax.broadcasted_iota(jnp.int32, (subs, slots), 1)
    live = (slot < count_ref[...]).astype(F32)
    vis_re = vis_ref[0] * live
    vis_im = vis_ref[1] * live
    coord_u = off_ref[0]
    coord_v = off_ref[1]
    step_u = unit_circle(coord_u * (8.0 / SUB))
    step_v = unit_circle(coord_v * (8.0 / SUB))
    first = (lax.broadcasted_iota(jnp.int32, (8, slots), 0) - SUB // 2).astype(F32) * (1.0 / SUB)
    for i in range(subs):
        row = slice(i, i + 1)

        def wide(value):
            return jnp.broadcast_to(value[row, :], (8, slots))

        def climb(re, im, step):
            step_re, step_im = wide(step[0]), wide(step[1])
            res, ims = [re], [im]
            for _ in range(SUB // 8 - 1):
                re, im = re * step_re - im * step_im, re * step_im + im * step_re
                res.append(re)
                ims.append(im)
            return jnp.concatenate(res + ims, axis=0).astype(BF16)

        cos_u, sin_u = unit_circle(wide(coord_u) * first)
        value_re, value_im = wide(vis_re), wide(vis_im)
        left = climb(value_re * cos_u - value_im * sin_u, value_re * sin_u + value_im * cos_u, step_u)
        cos_v, sin_v = unit_circle(wide(coord_v) * first)
        right = climb(cos_v, sin_v, step_v)
        both = lax.dot_general(left, right, (((1,), (1,)), ((), ())), preferred_element_type=F32)
        out_ref[0, i] = both[:SUB, :SUB] - both[SUB:, SUB:]
        out_ref[1, i] = both[:SUB, SUB:] + both[SUB:, :SUB]


def predict(visibility, uv_offset, vis_count):
    subs, slots = visibility.shape[1:]
    block = 8
    return pl.pallas_call(
        predict_kernel,
        grid=(subs // block,),
        in_specs=[
            pl.BlockSpec((2, block, slots), lambda i: (0, i, 0)),
            pl.BlockSpec((2, block, slots), lambda i: (0, i, 0)),
            pl.BlockSpec((block, 1), lambda i: (i, 0)),
        ],
        out_specs=pl.BlockSpec((2, block, SUB, SUB), lambda i: (0, i, 0, 0)),
        out_shape=jax.ShapeDtypeStruct((2, subs, SUB, SUB), F32),
        compiler_params=pltpu.CompilerParams(vmem_limit_bytes=48 << 20),
        cost_estimate=pl.CostEstimate(
            flops=subs * slots * 64 * 64 * 8, bytes_accessed=subs * slots * 16, transcendentals=0
        ),
        name="predict",
    )(visibility, uv_offset, vis_count.reshape(subs, 1))


def small_transform_table():
    centred = np.arange(SUB) - SUB // 2
    turns = np.outer(centred, centred) % SUB
    axis = np.exp(-2j * np.pi * turns / SUB)
    full = np.einsum("ap,bq->abpq", axis, axis).reshape(SUB, SUB, SUB * SUB) / SUB
    re, im = full.real, full.imag
    table = np.stack(
        [np.concatenate([re, -im], axis=2), np.concatenate([im, re], axis=2)], axis=1
    )
    return table.reshape(2 * SUB * SUB, 2 * SUB * SUB)


def column_table(owners, width):
    turns = np.outer(np.arange(N), np.arange(SUB)) % N
    wave = np.exp(2j * np.pi * turns / N).reshape(owners, width, SUB)
    table = np.concatenate(
        [
            np.concatenate([wave.real, -wave.imag], axis=2),
            np.concatenate([wave.imag, wave.real], axis=2),
        ],
        axis=1,
    )
    return np.concatenate(split_high_low(table), axis=2)


def tile_row_table():
    turns = np.outer(np.arange(TILES), np.arange(TILES)) % TILES
    wave = np.exp(2j * np.pi * turns / TILES)
    table = np.concatenate(
        [
            np.concatenate([wave.real, wave.imag], axis=1),
            np.concatenate([-wave.imag, wave.real], axis=1),
        ],
        axis=0,
    )
    high, low = split_high_low(table)
    return np.concatenate([high, high, low], axis=0)


def twiddle_table():
    turns = np.outer(np.arange(SUB), np.arange(TILES)) % N
    wave = np.exp(2j * np.pi * turns / N) / N
    return np.stack([wave.real, wave.imag], axis=1).astype(np.float32)


def fourier(res, ims):
    count = len(res)
    if count == 1:
        return res, ims
    even_re, even_im = fourier(res[0::2], ims[0::2])
    odd_re, odd_im = fourier(res[1::2], ims[1::2])
    low_re, low_im, high_re, high_im = [], [], [], []
    for k in range(count // 2):
        a, b = odd_re[k], odd_im[k]
        if k == 0:
            t_re, t_im = a, b
        elif 4 * k == count:
            t_re, t_im = -b, a
        elif 8 * k == count:
            t_re, t_im = (a - b) * math.sqrt(0.5), (a + b) * math.sqrt(0.5)
        elif 8 * k == 3 * count:
            t_re, t_im = (a + b) * -math.sqrt(0.5), (a - b) * math.sqrt(0.5)
        else:
            c, s = math.cos(2 * math.pi * k / count), math.sin(2 * math.pi * k / count)
            t_re, t_im = a * c - b * s, a * s + b * c
        low_re.append(even_re[k] + t_re)
        low_im.append(even_im[k] + t_im)
        high_re.append(even_re[k] - t_re)
        high_im.append(even_im[k] - t_im)
    return low_re + high_re, low_im + high_im


def image_kernel(
    uv_ref, wave_ref, cos_ref, sin_ref, hot_ref, rows_ref, twiddle_ref, sky_ref, shifted, middle
):
    step = pl.program_id(0)
    senders, subs = uv_ref.shape[0], uv_ref.shape[2]
    width = middle.shape[2]
    period = cos_ref.shape[0]
    together = min(senders, max(1, 256 // subs))

    @pl.when(step < SUB)
    def _():
        for begin in range(0, senders, together):
            uv = jnp.concatenate([uv_ref[d] for d in range(begin, begin + together)], axis=1)
            waves = jnp.dot(
                wave_ref[...],
                jnp.concatenate([uv, uv], axis=0),
                preferred_element_type=F32,
            )
            lanes = slice(begin * subs, (begin + together) * subs)
            cosine, sine = cos_ref[:, lanes], sin_ref[:, lanes]
            for at in range(0, width, period):
                re = waves[at : at + period]
                im = waves[width + at : width + at + period]
                shifted[at : at + period, lanes] = (re * cosine - im * sine).astype(BF16)
                shifted[width + at : width + at + period, lanes] = (
                    re * sine + im * cosine
                ).astype(BF16)
        placed = jnp.dot(shifted[...], hot_ref[...], preferred_element_type=F32)
        placed = jnp.concatenate([placed[:width], placed[width:]], axis=1)
        high = placed.astype(BF16)
        low = (placed - high.astype(F32)).astype(BF16)
        along = jnp.dot(
            jnp.concatenate([high, low, high], axis=1), rows_ref[...], preferred_element_type=F32
        )
        turn_re, turn_im = twiddle_ref[0:1, :], twiddle_ref[1:2, :]
        re, im = along[:, :TILES], along[:, TILES:]
        middle[0, step] = re * turn_re - im * turn_im
        middle[1, step] = re * turn_im + im * turn_re

    @pl.when(step >= SUB)
    def _():
        rows = sky_ref.shape[1]
        base = (step - SUB) * rows

        @pl.loop(0, rows // 8)
        def _(i):
            here = pl.ds(pl.multiple_of(i * 8, 8), 8)
            there = pl.ds(pl.multiple_of(base + i * 8, 8), 8)
            res, ims = fourier(
                [middle[0, a, there, :] for a in range(SUB)],
                [middle[1, a, there, :] for a in range(SUB)],
            )
            for k in range(SUB):
                sky_ref[0, here, k * TILES : (k + 1) * TILES] = res[k]
                sky_ref[1, here, k * TILES : (k + 1) * TILES] = ims[k]


def to_sky(uv, wave, cosine, sine, hot, rows, twiddle):
    senders, _, planes, subs = uv.shape
    width = wave.shape[0] // 2
    every = senders * subs
    block = min(32, width)

    def whole(array):
        return pl.BlockSpec(array.shape, lambda i: (0,) * array.ndim)

    return pl.pallas_call(
        image_kernel,
        grid=(SUB + width // block,),
        in_specs=[
            pl.BlockSpec((senders, None, planes, subs), lambda i: (0, jnp.minimum(i, SUB - 1), 0, 0)),
            whole(wave),
            whole(cosine),
            whole(sine),
            whole(hot),
            whole(rows),
            pl.BlockSpec((None, 2, TILES), lambda i: (jnp.minimum(i, SUB - 1), 0, 0)),
        ],
        out_specs=pl.BlockSpec((2, block, N), lambda i: (0, jnp.maximum(i - SUB, 0), 0)),
        out_shape=jax.ShapeDtypeStruct((2, width, N), F32),
        scratch_shapes=[
            pltpu.VMEM((2 * width, every), BF16),
            pltpu.VMEM((2, SUB, width, TILES), F32),
        ],
        compiler_params=pltpu.CompilerParams(vmem_limit_bytes=56 << 20),
        name="to_sky",
    )(uv, wave, cosine, sine, hot, rows, twiddle)


def shards(visibility, uv_offset, aterm, station_pair, tile_of, vis_count):
    subs = visibility.shape[1]
    owners = lax.axis_size("row") * lax.axis_size("stn")
    area = SUB * SUB
    width = N // owners
    me = lax.axis_index("row") * lax.axis_size("stn") + lax.axis_index("stn")

    tiles = lax.all_gather(tile_of, ("row", "stn"), axis=0, tiled=True)
    every_station = lax.all_gather(aterm, "stn", axis=1, tiled=True)
    image = predict(visibility, uv_offset, vis_count).reshape(2, subs, area)

    first = jnp.take(every_station, station_pair[:, 0], axis=1).astype(F32)
    second = jnp.take(every_station, station_pair[:, 1], axis=1).astype(F32)
    beam_re = first[0] * second[0] + first[1] * second[1]
    beam_im = first[1] * second[0] - first[0] * second[1]
    shaped = jnp.concatenate(
        [image[0] * beam_re - image[1] * beam_im, image[0] * beam_im + image[1] * beam_re], axis=1
    )
    shaped_high = lax.reduce_precision(shaped, 8, 7)
    shaped_low = (shaped - shaped_high).astype(BF16)
    shaped_high = shaped_high.astype(BF16)
    table_high, table_low = (jnp.asarray(t) for t in split_high_low(small_transform_table()))

    def product(table, data):
        return lax.dot_general(table, data, (((1,), (1,)), ((), ())), preferred_element_type=F32)

    uv = (
        product(table_high, shaped_high)
        + product(table_high, shaped_low)
        + product(table_low, shaped_high)
    ).astype(BF16)
    gathered = lax.all_gather(uv.reshape(SUB, 2 * SUB, subs), ("row", "stn"), axis=0)

    period = min(TILES, width)
    columns = (me * width + jnp.arange(period, dtype=jnp.int32)) % TILES
    turns = ((columns[:, None] * (tiles % TILES)[None, :]) % TILES).astype(F32) * (
        2.0 * math.pi / TILES
    )
    hot = ((tiles // TILES)[:, None] == jnp.arange(TILES, dtype=jnp.int32)[None, :]).astype(BF16)
    wave = lax.dynamic_index_in_dim(
        jnp.asarray(column_table(owners, width)), me, axis=0, keepdims=False
    )
    return to_sky(
        gathered,
        wave,
        jnp.cos(turns),
        jnp.sin(turns),
        hot,
        jnp.asarray(tile_row_table()),
        jnp.asarray(twiddle_table()),
    )


def solution(mesh):
    in_specs = (
        P(None, ("chan", "row", "stn"), None),
        P(None, ("chan", "row", "stn"), None),
        P(None, ("chan", "stn"), None),
        P(("chan", "row", "stn"), None),
        P(("chan", "row", "stn")),
        P(("chan", "row", "stn")),
    )
    out_specs = P("chan", ("row", "stn"), None)
    return jax.shard_map(shards, mesh=mesh, in_specs=in_specs, out_specs=out_specs, check_vma=False)
```

```python
import math

import jax
import jax.numpy as jnp
import ml_dtypes
import numpy as np
from jax import lax
from jax.experimental import pallas as pl
from jax.experimental.pallas import tpu as pltpu
from jax.sharding import PartitionSpec as P

N = 4096
SUB = 32
TILES = N // SUB
BF16 = jnp.bfloat16
F32 = jnp.float32

SIN_POLY = tuple((-1) ** k * math.pi ** (2 * k + 1) / math.factorial(2 * k + 1) for k in range(6))
COS_POLY = tuple((-1) ** k * math.pi ** (2 * k) / math.factorial(2 * k) for k in range(7))


def unit_circle(turns):
    part = turns - jnp.round(turns)
    square = part * part
    sine = SIN_POLY[-1]
    for coefficient in SIN_POLY[-2::-1]:
        sine = sine * square + coefficient
    sine = sine * part
    cosine = COS_POLY[-1]
    for coefficient in COS_POLY[-2::-1]:
        cosine = cosine * square + coefficient
    return 1.0 - 2.0 * sine * sine, 2.0 * sine * cosine


def split_high_low(table):
    high = table.astype(ml_dtypes.bfloat16)
    low = (table - high.astype(np.float64)).astype(ml_dtypes.bfloat16)
    return high, low


def predict_kernel(vis_ref, off_ref, count_ref, out_ref):
    subs, slots = vis_ref.shape[1], vis_ref.shape[2]
    slot = lax.broadcasted_iota(jnp.int32, (subs, slots), 1)
    live = (slot < count_ref[...]).astype(F32)
    vis_re = vis_ref[0] * live
    vis_im = vis_ref[1] * live
    coord_u = off_ref[0]
    coord_v = off_ref[1]
    step_u = unit_circle(coord_u * (8.0 / SUB))
    step_v = unit_circle(coord_v * (8.0 / SUB))
    first = (lax.broadcasted_iota(jnp.int32, (8, slots), 0) - SUB // 2).astype(F32) * (1.0 / SUB)
    for i in range(subs):
        row = slice(i, i + 1)

        def wide(value):
            return jnp.broadcast_to(value[row, :], (8, slots))

        def climb(re, im, step):
            step_re, step_im = wide(step[0]), wide(step[1])
            res, ims = [re], [im]
            for _ in range(SUB // 8 - 1):
                re, im = re * step_re - im * step_im, re * step_im + im * step_re
                res.append(re)
                ims.append(im)
            return jnp.concatenate(res + ims, axis=0).astype(BF16)

        cos_u, sin_u = unit_circle(wide(coord_u) * first)
        value_re, value_im = wide(vis_re), wide(vis_im)
        left = climb(value_re * cos_u - value_im * sin_u, value_re * sin_u + value_im * cos_u, step_u)
        cos_v, sin_v = unit_circle(wide(coord_v) * first)
        right = climb(cos_v, sin_v, step_v)
        both = lax.dot_general(left, right, (((1,), (1,)), ((), ())), preferred_element_type=F32)
        out_ref[0, i] = both[:SUB, :SUB] - both[SUB:, SUB:]
        out_ref[1, i] = both[:SUB, SUB:] + both[SUB:, :SUB]


def predict(visibility, uv_offset, vis_count):
    subs, slots = visibility.shape[1:]
    block = 8
    return pl.pallas_call(
        predict_kernel,
        grid=(subs // block,),
        in_specs=[
            pl.BlockSpec((2, block, slots), lambda i: (0, i, 0)),
            pl.BlockSpec((2, block, slots), lambda i: (0, i, 0)),
            pl.BlockSpec((block, 1), lambda i: (i, 0)),
        ],
        out_specs=pl.BlockSpec((2, block, SUB, SUB), lambda i: (0, i, 0, 0)),
        out_shape=jax.ShapeDtypeStruct((2, subs, SUB, SUB), F32),
        compiler_params=pltpu.CompilerParams(vmem_limit_bytes=48 << 20),
        cost_estimate=pl.CostEstimate(
            flops=subs * slots * 64 * 64 * 8, bytes_accessed=subs * slots * 16, transcendentals=0
        ),
        name="predict",
    )(visibility, uv_offset, vis_count.reshape(subs, 1))


def small_transform_table():
    centred = np.arange(SUB) - SUB // 2
    turns = np.outer(centred, centred) % SUB
    axis = np.exp(-2j * np.pi * turns / SUB)
    full = np.einsum("ap,bq->abpq", axis, axis).reshape(SUB, SUB, SUB * SUB) / SUB
    re, im = full.real, full.imag
    table = np.stack(
        [np.concatenate([re, -im], axis=2), np.concatenate([im, re], axis=2)], axis=1
    )
    return table.reshape(2 * SUB * SUB, 2 * SUB * SUB)


def column_table(owners, width):
    turns = np.outer(np.arange(N), np.arange(SUB)) % N
    wave = np.exp(2j * np.pi * turns / N).reshape(owners, width, SUB)
    table = np.concatenate(
        [
            np.concatenate([wave.real, -wave.imag], axis=2),
            np.concatenate([wave.imag, wave.real], axis=2),
        ],
        axis=1,
    )
    return np.concatenate(split_high_low(table), axis=2)


def twiddle_table():
    turns = np.outer(np.arange(SUB), np.arange(TILES)) % N
    wave = np.exp(2j * np.pi * turns / N) / N
    return np.stack([wave.real, wave.imag], axis=1).astype(np.float32)


def fourier(res, ims):
    count = len(res)
    if count == 1:
        return res, ims
    even_re, even_im = fourier(res[0::2], ims[0::2])
    odd_re, odd_im = fourier(res[1::2], ims[1::2])
    low_re, low_im, high_re, high_im = [], [], [], []
    for k in range(count // 2):
        a, b = odd_re[k], odd_im[k]
        if k == 0:
            t_re, t_im = a, b
        elif 4 * k == count:
            t_re, t_im = -b, a
        elif 8 * k == count:
            t_re, t_im = (a - b) * math.sqrt(0.5), (a + b) * math.sqrt(0.5)
        elif 8 * k == 3 * count:
            t_re, t_im = (a + b) * -math.sqrt(0.5), (a - b) * math.sqrt(0.5)
        else:
            c, s = math.cos(2 * math.pi * k / count), math.sin(2 * math.pi * k / count)
            t_re, t_im = a * c - b * s, a * s + b * c
        low_re.append(even_re[k] + t_re)
        low_im.append(even_im[k] + t_im)
        high_re.append(even_re[k] - t_re)
        high_im.append(even_im[k] - t_im)
    return low_re + high_re, low_im + high_im


def columns_of_one_row(uv_ref, wave_ref, cos_ref, sin_ref, rows_ref, twiddle_ref, shifted):
    senders, subs = uv_ref.shape[0], uv_ref.shape[2]
    width, every = shifted.shape[0], shifted.shape[1] // 2
    period = cos_ref.shape[0]
    together = min(senders, max(1, 256 // subs))
    for begin in range(0, senders, together):
        uv = jnp.concatenate([uv_ref[d] for d in range(begin, begin + together)], axis=1)
        waves = jnp.dot(
            wave_ref[...], jnp.concatenate([uv, uv], axis=0), preferred_element_type=F32
        )
        first, last = begin * subs, (begin + together) * subs
        cosine, sine = cos_ref[:, first:last], sin_ref[:, first:last]
        for at in range(0, width, period):
            re = waves[at : at + period]
            im = waves[width + at : width + at + period]
            shifted[at : at + period, first:last] = (re * cosine - im * sine).astype(BF16)
            shifted[at : at + period, every + first : every + last] = (
                re * sine + im * cosine
            ).astype(BF16)
    along = jnp.dot(shifted[...], rows_ref[...], preferred_element_type=F32)
    turn_re, turn_im = twiddle_ref[0:1, :], twiddle_ref[1:2, :]
    re, im = along[:, :TILES], along[:, TILES:]
    return re * turn_re - im * turn_im, re * turn_im + im * turn_re


def early_kernel(*refs):
    *inputs, middle_ref, shifted = refs
    middle_ref[0], middle_ref[1] = columns_of_one_row(*inputs, shifted)


def late_kernel(*refs):
    *inputs, early_ref, sky_ref, shifted, middle = refs
    step = pl.program_id(0)
    steps = middle.shape[1]

    @pl.when(step < steps)
    def _():
        middle[0, step], middle[1, step] = columns_of_one_row(*inputs, shifted)

    @pl.when(step >= steps)
    def _():
        rows = sky_ref.shape[1]
        base = (step - steps) * rows

        @pl.loop(0, rows // 8)
        def _(i):
            here = pl.ds(pl.multiple_of(i * 8, 8), 8)
            there = pl.ds(pl.multiple_of(base + i * 8, 8), 8)
            res, ims = fourier(
                *(
                    [early_ref[c, a, here, :] for a in range(SUB - steps)]
                    + [middle[c, a, there, :] for a in range(steps)]
                    for c in range(2)
                )
            )
            for k in range(SUB):
                sky_ref[0, here, k * TILES : (k + 1) * TILES] = res[k]
                sky_ref[1, here, k * TILES : (k + 1) * TILES] = ims[k]


def step_specs(uv, wave, cosine, sine, rows, twiddle, begin, steps):
    senders, _, planes, subs = uv.shape

    def whole(array):
        return pl.BlockSpec(array.shape, lambda i: (0,) * array.ndim)

    return [
        pl.BlockSpec((senders, None, planes, subs), lambda i: (0, jnp.minimum(i, steps - 1), 0, 0)),
        whole(wave),
        whole(cosine),
        whole(sine),
        whole(rows),
        pl.BlockSpec((None, 2, TILES), lambda i: (begin + jnp.minimum(i, steps - 1), 0, 0)),
    ]


def early_rows(uv, *tables):
    senders, steps, _, subs = uv.shape
    width = tables[0].shape[0] // 2
    every = senders * subs
    return pl.pallas_call(
        early_kernel,
        grid=(steps,),
        in_specs=step_specs(uv, *tables, 0, steps),
        out_specs=pl.BlockSpec((2, None, width, TILES), lambda i: (0, i, 0, 0)),
        out_shape=jax.ShapeDtypeStruct((2, steps, width, TILES), F32),
        scratch_shapes=[pltpu.VMEM((width, 2 * every), BF16)],
        compiler_params=pltpu.CompilerParams(vmem_limit_bytes=56 << 20),
        cost_estimate=pl.CostEstimate(
            flops=steps * 4 * every * width * 1024, bytes_accessed=16 << 20, transcendentals=0
        ),
        name="early_rows",
    )(uv, *tables)


def late_rows_to_sky(uv, *tables_and_early):
    *tables, early = tables_and_early
    senders, steps, _, subs = uv.shape
    width = tables[0].shape[0] // 2
    every = senders * subs
    block = min(32, width)
    return pl.pallas_call(
        late_kernel,
        grid=(steps + width // block,),
        in_specs=step_specs(uv, *tables, SUB - steps, steps)
        + [
            pl.BlockSpec(
                (2, SUB - steps, block, TILES), lambda i: (0, 0, jnp.maximum(i - steps, 0), 0)
            )
        ],
        out_specs=pl.BlockSpec((2, block, N), lambda i: (0, jnp.maximum(i - steps, 0), 0)),
        out_shape=jax.ShapeDtypeStruct((2, width, N), F32),
        scratch_shapes=[
            pltpu.VMEM((width, 2 * every), BF16),
            pltpu.VMEM((2, steps, width, TILES), F32),
        ],
        compiler_params=pltpu.CompilerParams(vmem_limit_bytes=56 << 20),
        name="late_rows_to_sky",
    )(uv, *tables, early)


def stations_and_places(aterm, pairs):
    here = aterm.shape[1]
    rows, sides = lax.axis_size("row"), lax.axis_size("stn")
    if sides != 2 or rows % 2 or here % 2:
        return lax.all_gather(aterm, "stn", axis=1, tiled=True), pairs
    half = here // 2
    parity = lax.axis_index("row") % 2
    mine = lax.dynamic_slice_in_dim(aterm, parity * half, half, 1)
    fetched = lax.ppermute(mine, "stn", [(0, 1), (1, 0)])
    passed = lax.ppermute(fetched, "row", [(i, i ^ 1) for i in range(rows)])
    own = pairs // here == lax.axis_index("stn")
    inside = pairs % here
    far = here + jnp.where(inside // half == parity, 0, half) + inside % half
    return jnp.concatenate([aterm, fetched, passed], axis=1), jnp.where(own, inside, far)


def shards(visibility, uv_offset, aterm, station_pair, tile_of, vis_count):
    subs = visibility.shape[1]
    owners = lax.axis_size("row") * lax.axis_size("stn")
    area = SUB * SUB
    width = N // owners
    me = lax.axis_index("row") * lax.axis_size("stn") + lax.axis_index("stn")

    tiles = lax.all_gather(tile_of, ("row", "stn"), axis=0, tiled=True)
    every_station, places = stations_and_places(aterm, station_pair)
    image = predict(visibility, uv_offset, vis_count).reshape(2, subs, area)

    first = jnp.take(every_station, places[:, 0], axis=1).astype(F32)
    second = jnp.take(every_station, places[:, 1], axis=1).astype(F32)
    beam_re = first[0] * second[0] + first[1] * second[1]
    beam_im = first[1] * second[0] - first[0] * second[1]
    shaped = jnp.concatenate(
        [image[0] * beam_re - image[1] * beam_im, image[0] * beam_im + image[1] * beam_re], axis=1
    )
    shaped_high = lax.reduce_precision(shaped, 8, 7)
    shaped_low = (shaped - shaped_high).astype(BF16)
    shaped_high = shaped_high.astype(BF16)
    table_high, table_low = (jnp.asarray(t) for t in split_high_low(small_transform_table()))

    def product(table, data):
        return lax.dot_general(table, data, (((1,), (1,)), ((), ())), preferred_element_type=F32)

    uv = (
        product(table_high, shaped_high)
        + product(table_high, shaped_low)
        + product(table_low, shaped_high)
    ).astype(BF16)
    uv = uv.reshape(SUB, 2 * SUB, subs)
    cut = 3 * SUB // 8
    uv_early = lax.all_gather(uv[:cut], ("row", "stn"), axis=0)

    period = min(TILES, width)
    columns = (me * width + jnp.arange(period, dtype=jnp.int32)) % TILES
    turns = ((columns[:, None] * (tiles % TILES)[None, :]) % TILES).astype(F32) * (
        2.0 * math.pi / TILES
    )
    lines = jnp.arange(TILES, dtype=jnp.int32)
    row_turns = (((tiles // TILES)[:, None] * lines[None, :]) % TILES).astype(F32) * (
        2.0 * math.pi / TILES
    )
    row_cos, row_sin = jnp.cos(row_turns), jnp.sin(row_turns)
    rows = jnp.concatenate(
        [
            jnp.concatenate([row_cos, row_sin], axis=1),
            jnp.concatenate([-row_sin, row_cos], axis=1),
        ],
        axis=0,
    ).astype(BF16)
    wave = lax.dynamic_index_in_dim(
        jnp.asarray(column_table(owners, width)), me, axis=0, keepdims=False
    )
    tables = (wave, jnp.cos(turns), jnp.sin(turns), rows, jnp.asarray(twiddle_table()))
    uv_rest, tables = lax.optimization_barrier((uv[cut:], tables))
    uv_late = lax.all_gather(uv_rest, ("row", "stn"), axis=0)
    early = early_rows(uv_early, *tables)
    return late_rows_to_sky(uv_late, *tables, early)


def solution(mesh):
    in_specs = (
        P(None, ("chan", "row", "stn"), None),
        P(None, ("chan", "row", "stn"), None),
        P(None, ("chan", "stn"), None),
        P(("chan", "row", "stn"), None),
        P(("chan", "row", "stn")),
        P(("chan", "row", "stn")),
    )
    out_specs = P("chan", ("row", "stn"), None)
    return jax.shard_map(shards, mesh=mesh, in_specs=in_specs, out_specs=out_specs, check_vma=False)
```
